128 devices in a mesh: section: 8 (over x_hi, z), seq: 16 (over x_lo, y, core).
Axes of the slice: x: 4 (x_hi: 2, x_lo: 2; x = x_hi * 2 + x_lo), y: 4, z: 4, core: 2. Of those that a mesh axis runs over, the one named last changes fastest.
Arguments:
- queries: bfloat16 [8, 1536, 6144], P('section', 'seq'), may hold values from -140 to 140
- keys: bfloat16 [8, 1536, 6144], P('section', 'seq'), may hold values from -7 to 7
- values: bfloat16 [8, 1536, 6144], P('section', 'seq'), may hold values from -24 to 24
- lengths: int32 [8], replicated, may hold values from 768 to 1536, as said below
- span_mask: int32 [8, 8], replicated, may hold values from 0 to 1, as said below
Outputs:
- shifted: bfloat16 [8, 1536, 6144], P('section', 'seq')
The draws below stay inside these ranges and needn't reach their ends.
Inputs may be any that keep to these rules, and one draw needn't show every extreme that they name: `lengths`: each entry lies from 768 to 1536; some group has exactly 1536. `span_mask`: ones on the diagonal, zeros above it; a row s has ones only in columns s - 4 to s; row 7 has a one in column 3.
All inputs are finite; a program needn't handle non-finite values.
Results may differ from the reference program's by a relative error of at most 0.0065.
Values may be sent and summed in bfloat16 or wider, within the bound.
No kernel may reach another device: no remote copies, remote signals or barrier semaphores. Data moves between devices by JAX's collectives and lax.ppermute only.
A program may use at most 128 MiB of HBM per device.

```python
import jax
import jax.numpy as jnp
from jax import lax

D = 6144
HEADS = 48
HEAD = 128
CTX = 5
GROUP = 1536
LEVELS = 8


def shared_keys(key):
    return jnp.clip(jax.random.normal(jax.random.fold_in(key, 11), (LEVELS, GROUP, D), jnp.float32), -6.0, 6.0)


def draw_keys(key, part):
    base = shared_keys(key)
    return base.astype(jnp.bfloat16)


def draw_queries(key, part):
    key = jax.random.fold_in(key, 2)
    return jnp.clip(0.5 * jax.random.normal(key, (LEVELS, GROUP, D), jnp.float32), -3.0, 3.0).astype(jnp.bfloat16)


def draw_lengths(key, part):
    key = jax.random.fold_in(key, 3)
    drawn = jax.random.randint(jax.random.fold_in(key, 1), (LEVELS,), GROUP // 2, GROUP + 1)
    where_full = jax.random.randint(jax.random.fold_in(key, 2), (), 0, LEVELS)
    return jnp.where(jnp.arange(LEVELS) == where_full, GROUP, drawn).astype(jnp.int32)


def draw_span_mask(key, part):
    key = jax.random.fold_in(key, 4)
    rows = jnp.arange(LEVELS)[:, None]
    cols = jnp.arange(LEVELS)[None, :]
    band = (cols <= rows) & (cols > rows - CTX)
    coins = jax.random.randint(key, (LEVELS, LEVELS), 0, 2)
    far = (rows == LEVELS - 1) & (cols == LEVELS - 1 - LEVELS // 2)
    pick = (cols == rows) | far | (coins > 0)
    return jnp.where(band & pick, 1, 0).astype(jnp.int32)


def block_levels(key, extent, shards, low, largest):
    level = 1.0
    for position, shards_of in shards:
        steps = jax.random.uniform(jax.random.fold_in(jax.random.fold_in(key, 6), position), (shards_of,), jnp.float32, low / len(shards), largest / len(shards))
        level = level * jnp.repeat(jnp.exp(steps), extent[position] // shards_of).reshape((-1,) + (1,) * (len(extent) - 1 - position))
    return level


def normal_values(own_key, dims, deviation, limit, split=(), held_as=jnp.bfloat16):
    values = jax.random.normal(own_key, dims, jnp.float32) * deviation
    if len(split) > 0:
        values = block_levels(own_key, dims, split, -0.22, 0.18) * values
    return jnp.clip(values, min=-limit, max=limit).astype(held_as)


def setup_inputs(seed: int = 0) -> dict:
    key_of = jax.random.split(jax.random.key(seed), 6)
    queries = draw_queries(jax.random.fold_in(key_of[5], 71), 0)
    keys = draw_keys(jax.random.fold_in(key_of[5], 71), 0)
    values = normal_values(key_of[2], (LEVELS, GROUP, D), 4.0, 24.0, ((0, 8), (1, 16)))
    lengths = draw_lengths(jax.random.fold_in(key_of[5], 71), 0)
    span_mask = draw_span_mask(jax.random.fold_in(key_of[5], 71), 0)
    return {"queries": queries, "keys": keys, "values": values, "lengths": lengths, "span_mask": span_mask}


def reference(queries, keys, values, lengths, span_mask):
    scale = HEAD ** -0.5
    slots = jnp.arange(GROUP)
    results = []
    for level_now in range(LEVELS):
        count = level_now + 1
        live = (span_mask[level_now, :count][:, None] > 0) & (slots[None, :] < lengths[:count][:, None])
        live = live.reshape(count * GROUP)
        query_heads = jnp.transpose(queries[level_now].reshape(GROUP, HEADS, HEAD), (1, 0, 2))
        key_heads = jnp.transpose(keys[:count].reshape(count * GROUP, HEADS, HEAD), (1, 0, 2))
        value_heads = jnp.transpose(values[:count].reshape(count * GROUP, HEADS, HEAD), (1, 0, 2))

        def one_head(operands):
            query_one, key_one, value_one = operands
            score = jnp.dot(query_one, key_one.T, preferred_element_type=jnp.float32) * scale
            score = jnp.where(live[None, :], score, -jnp.inf)
            top = jnp.max(score, axis=1, keepdims=True)
            expo = jnp.exp(score - top)
            total = jnp.sum(expo, axis=1, keepdims=True)
            numer = jnp.dot(expo.astype(jnp.bfloat16), value_one, preferred_element_type=jnp.float32)
            return (numer / total).astype(jnp.bfloat16)

        attended = lax.map(one_head, (query_heads, key_heads, value_heads))
        results.append(jnp.transpose(attended, (1, 0, 2)).reshape(GROUP, D))
    attended_all = jnp.stack(results)
    return jnp.roll(attended_all, 1, axis=0)
```

```python
import jax
import jax.numpy as jnp
from jax import lax
from jax.experimental import pallas as pl
from jax.experimental.pallas import tpu as pltpu
from jax.sharding import PartitionSpec as P

HEAD = 128
LOG2E = 1.4426950408889634
BLOCK_Q = 768
KEY_STEP = 256
REACH = 5
CORES = 2


def attend(lengths, span_mask, active, queries, keys_even, keys_odd, values_even, values_odd):
    groups, rows, _ = queries.shape
    run = 96
    span = CORES * rows
    sizes = [n for n in range(KEY_STEP, span + 1, KEY_STEP) if n >= span // 2]

    def kernel(len_ref, mask_ref, active_ref, q_ref, k0_ref, k1_ref, v0_ref, v1_ref, o_ref, keys, values, top, acc):
        def stage(c, carry):
            count = len_ref[c]
            first = k0_ref[c, 0:1, :]
            for h, (k_ref, v_ref) in enumerate(((k0_ref, v0_ref), (k1_ref, v1_ref))):
                for i in range(rows // run):
                    base = (CORES * i + h) * run
                    live = (base + lax.broadcasted_iota(jnp.int32, (run, HEAD), 0)) < count
                    here = slice(base, base + run)
                    there = slice(i * run, (i + 1) * run)
                    keys[c, here, :] = jnp.where(live, k_ref[c, there, :], first)
                    values[c, here, 0:HEAD] = jnp.where(live, v_ref[c, there, :], jnp.bfloat16(0))
                    values[c, here, HEAD:] = jnp.where(live, jnp.bfloat16(1), jnp.bfloat16(0))
            return carry

        def step(q, c, n, fresh):
            k = keys[c, 0:n, :]
            score = lax.dot_general(
                q,
                jnp.concatenate([k, k], axis=1),
                (((1,), (1,)), ((), ())),
                preferred_element_type=jnp.float32,
            )
            new_top = jnp.max(score, axis=1, keepdims=True)
            if not fresh:
                old_top = top[:, 0:1]
                new_top = jnp.maximum(old_top, new_top)
            weight = jnp.exp2(score - new_top).astype(jnp.bfloat16)
            update = jnp.dot(weight, values[c, 0:n, :], preferred_element_type=jnp.float32)
            if fresh:
                acc[...] = update
            else:
                acc[...] = acc[...] * jnp.exp2(old_top - new_top) + update
            top[...] = jnp.broadcast_to(new_top, top.shape)

        def by_length(q, c, fresh):
            steps = (len_ref[c] + KEY_STEP - 1) // KEY_STEP
            for n in sizes:
                pl.when(steps == n // KEY_STEP)(lambda n=n: step(q, c, n, fresh))

        def one_block(t, carry):
            s = t // (rows // BLOCK_Q)
            here = pl.ds((t % (rows // BLOCK_Q)) * BLOCK_Q, BLOCK_Q)
            scaled = q_ref[s, here, :].astype(jnp.float32) * (LOG2E * HEAD**-0.5)
            high = scaled.astype(jnp.bfloat16)
            low = (scaled - high.astype(jnp.float32)).astype(jnp.bfloat16)
            q = jnp.concatenate([high, low], axis=1)
            by_length(q, s, True)

            def earlier(c, inner):
                pl.when(mask_ref[s, c] > 0)(lambda: by_length(q, c, False))
                return inner

            lax.fori_loop(jnp.maximum(s - (REACH - 1), 0), s, earlier, 0)
            total = acc[...]
            o_ref[lax.rem(s + 1, groups), here, :] = (total[:, :HEAD] / total[:, HEAD:]).astype(jnp.bfloat16)
            return carry

        @pl.when(active_ref[0] > 0)
        def _():
            lax.fori_loop(0, groups, stage, 0)
            lax.fori_loop(0, groups * (rows // BLOCK_Q), one_block, 0)

    smem = pl.BlockSpec(memory_space=pltpu.SMEM)
    vmem = pl.BlockSpec(memory_space=pltpu.VMEM)
    return pl.pallas_call(
        kernel,
        out_shape=jax.ShapeDtypeStruct(queries.shape, jnp.bfloat16),
        in_specs=[smem] * 3 + [vmem] * 5,
        out_specs=vmem,
        scratch_shapes=[
            pltpu.VMEM((groups, span, HEAD), jnp.bfloat16),
            pltpu.VMEM((groups, span, 2 * HEAD), jnp.bfloat16),
            pltpu.VMEM((BLOCK_Q, HEAD), jnp.float32),
            pltpu.VMEM((BLOCK_Q, 2 * HEAD), jnp.float32),
        ],
        compiler_params=pltpu.CompilerParams(vmem_limit_bytes=56 * 2**20),
        name="attend",
    )(lengths, span_mask, active, queries, keys_even, keys_odd, values_even, values_odd)


CHIPS = ("xh", "z", "xl", "y")


def body(queries, keys, values, lengths, span_mask):
    tokens, width = queries.shape[1:]
    heads = width // HEAD
    chips = lax.axis_size(CHIPS)
    groups = span_mask.shape[0]
    runs = chips // groups
    core = lax.axis_index("core")

    def by_head(array):
        return jnp.transpose(array[0].reshape(tokens, heads, HEAD), (1, 0, 2))

    sent = jnp.stack([by_head(queries), by_head(keys), by_head(values)], axis=1)
    sent = jnp.pad(sent, ((0, chips - heads), (0, 0), (0, 0), (0, 0)))
    got = lax.all_to_all(sent, CHIPS, 0, 0, tiled=True)

    def whole(i):
        return got[:, i].reshape(groups, runs * tokens, HEAD)

    own = jnp.stack([whole(1), whole(2)])
    other = lax.ppermute(own, "core", [(0, 1), (1, 0)])
    even, odd = jnp.where(core == 0, own, other), jnp.where(core == 0, other, own)
    active = (lax.axis_index(CHIPS) < heads).astype(jnp.int32).reshape(1)
    out = attend(lengths, span_mask, active, whole(0), even[0], odd[0], even[1], odd[1])
    back = lax.all_to_all(out.reshape(chips, tokens, HEAD), CHIPS, 0, 0, tiled=True)[:heads]
    return jnp.transpose(back, (1, 0, 2)).reshape(1, tokens, width)


def solution(mesh):
    fine = jax.sharding.Mesh(mesh.devices.reshape(2, 4, 2, 4, 2), ("xh", "z", "xl", "y", "core"))
    spec = P(("xh", "z"), ("xl", "y", "core"), None)
    return jax.shard_map(
        body,
        mesh=fine,
        in_specs=(spec, spec, spec, P(), P()),
        out_specs=spec,
        check_vma=False,
    )
```

```python
import jax
import jax.numpy as jnp
from jax import lax
from jax.experimental import pallas as pl
from jax.experimental.pallas import tpu as pltpu
from jax.sharding import PartitionSpec as P

HEAD = 128
LOG2E = 1.4426950408889634
BLOCK_Q = 384
KEY_STEP = 256
REACH = 5
CORES = 2


def attend(lengths, span_mask, place, got, other):
    groups = span_mask.shape[0]
    run = got.shape[2]
    runs = got.shape[0] // groups
    rows = runs * run
    span = CORES * rows
    sizes = [n for n in range(KEY_STEP, span + 1, KEY_STEP) if n >= span // 2]

    def kernel(len_ref, mask_ref, place_ref, got_ref, other_ref, o_ref, q_in, keys, values, ones, q, top, acc, sems):
        core = place_ref[1]
        by_run = (groups, runs, CORES, run, HEAD)
        keys_by_run, values_by_run = keys.reshape(by_run), values.reshape(by_run)

        def copies(c):
            here = pl.ds(c * runs, runs)
            pairs = (
                (got_ref.at[here, 0], q_in.at[c]),
                (got_ref.at[here, 1], keys_by_run.at[c, :, core]),
                (got_ref.at[here, 2], values_by_run.at[c, :, core]),
                (other_ref.at[here, 0], keys_by_run.at[c, :, 1 - core]),
                (other_ref.at[here, 1], values_by_run.at[c, :, 1 - core]),
            )
            return [pltpu.make_async_copy(src, dst, sems.at[c, i]) for i, (src, dst) in enumerate(pairs)]

        def start(c, carry):
            for copy in copies(c):
                copy.start()
            return carry

        def clean(c):
            count = len_ref[c]
            base = (count - 1) // KEY_STEP * KEY_STEP
            here = pl.ds(pl.multiple_of(c * span + base, KEY_STEP), KEY_STEP)
            live = (base + lax.broadcasted_iota(jnp.int32, (KEY_STEP, HEAD), 0)) < count
            first = keys[pl.ds(pl.multiple_of(c * span, KEY_STEP), 16), :][0:1]
            keys[here, :] = jnp.where(live, keys[here, :], first)
            values[here, :] = jnp.where(live, values[here, :], jnp.bfloat16(0))
            ones[here, :] = jnp.where(live, jnp.bfloat16(1), jnp.bfloat16(0))

        def step(c, n, fresh):
            here = pl.ds(pl.multiple_of(c * span, KEY_STEP), n)
            k = keys[here, :]
            k = jnp.concatenate([k, k], axis=1)
            v = jnp.concatenate([values[here, :], ones[here, :]], axis=1)

            def scores(i):
                return lax.dot_general(
                    q[i * BLOCK_Q : (i + 1) * BLOCK_Q, :],
                    k,
                    (((1,), (1,)), ((), ())),
                    preferred_element_type=jnp.float32,
                )

            later = scores(0)
            for i in range(rows // BLOCK_Q):
                block = slice(i * BLOCK_Q, (i + 1) * BLOCK_Q)
                score = later
                if i + 1 < rows // BLOCK_Q:
                    later = scores(i + 1)
                new_top = jnp.max(score, axis=1, keepdims=True)
                if not fresh:
                    old_top = top[block, 0:1]
                    new_top = jnp.maximum(old_top, new_top)
                weight = jnp.exp2(score - new_top).astype(jnp.bfloat16)
                update = jnp.dot(weight, v, preferred_element_type=jnp.float32)
                if fresh:
                    acc[block, :] = update
                else:
                    acc[block, :] = acc[block, :] * jnp.exp2(old_top - new_top) + update
                top[block, :] = jnp.broadcast_to(new_top, (BLOCK_Q, HEAD))

        def by_length(c, fresh):
            steps = (len_ref[c] + KEY_STEP - 1) // KEY_STEP
            for n in sizes:
                pl.when(steps == n // KEY_STEP)(lambda n=n: step(c, n, fresh))

        def one_group(s, carry):
            for copy in copies(s):
                copy.wait()
            clean(s)
            scaled = q_in[s].reshape(rows, HEAD).astype(jnp.float32) * (LOG2E * HEAD**-0.5)
            high = scaled.astype(jnp.bfloat16)
            q[:, :HEAD] = high
            q[:, HEAD:] = (scaled - high.astype(jnp.float32)).astype(jnp.bfloat16)
            by_length(s, True)

            def earlier(c, inner):
                pl.when(mask_ref[s, c] > 0)(lambda: by_length(c, False))
                return inner

            lax.fori_loop(jnp.maximum(s - (REACH - 1), 0), s, earlier, 0)
            total = acc[...]
            o_ref[lax.rem(s + 1, groups)] = (total[:, :HEAD] / total[:, HEAD:]).astype(jnp.bfloat16)
            return carry

        @pl.when(place_ref[0] > 0)
        def _():
            lax.fori_loop(0, groups, start, 0)
            ones[...] = jnp.ones(ones.shape, jnp.bfloat16)
            lax.fori_loop(0, groups, one_group, 0)

    smem = pl.BlockSpec(memory_space=pltpu.SMEM)
    where_it_is = pl.BlockSpec(memory_space=pl.ANY)
    bf16, f32 = jnp.bfloat16, jnp.float32
    return pl.pallas_call(
        kernel,
        out_shape=jax.ShapeDtypeStruct((groups, rows, HEAD), bf16),
        in_specs=[smem] * 3 + [where_it_is] * 2,
        out_specs=pl.BlockSpec(memory_space=pltpu.VMEM),
        scratch_shapes=[
            pltpu.VMEM((groups, runs, run, HEAD), bf16),
            pltpu.VMEM((groups * span, HEAD), bf16),
            pltpu.VMEM((groups * span, HEAD), bf16),
            pltpu.VMEM((groups * span, HEAD), bf16),
            pltpu.VMEM((rows, 2 * HEAD), bf16),
            pltpu.VMEM((rows, HEAD), f32),
            pltpu.VMEM((rows, 2 * HEAD), f32),
            pltpu.SemaphoreType.DMA((groups, 5)),
        ],
        compiler_params=pltpu.CompilerParams(vmem_limit_bytes=48 * 2**20),
        name="attend",
    )(lengths, span_mask, place, got, other)


CHIPS = ("xh", "z", "xl", "y")


def body(queries, keys, values, lengths, span_mask):
    tokens, width = queries.shape[1:]
    heads = width // HEAD
    chips = lax.axis_size(CHIPS)
    core = lax.axis_index("core")

    def by_head(array):
        return jnp.transpose(array[0].reshape(tokens, heads, HEAD), (1, 0, 2))

    sent = jnp.stack([by_head(queries), by_head(keys), by_head(values)], axis=1)
    sent = jnp.pad(sent, ((0, chips - heads), (0, 0), (0, 0), (0, 0)))
    got = lax.all_to_all(sent, CHIPS, 0, 0, tiled=True)

    other = lax.ppermute(got[:, 1:], "core", [(0, 1), (1, 0)])
    active = (lax.axis_index(CHIPS) < heads).astype(jnp.int32)
    out = attend(lengths, span_mask, jnp.stack([active, core]), got, other)
    back = lax.all_to_all(out.reshape(chips, tokens, HEAD), CHIPS, 0, 0, tiled=True)[:heads]
    return jnp.transpose(back, (1, 0, 2)).reshape(1, tokens, width)


def solution(mesh):
    fine = jax.sharding.Mesh(mesh.devices.reshape(2, 4, 2, 4, 2), ("xh", "z", "xl", "y", "core"))
    spec = P(("xh", "z"), ("xl", "y", "core"), None)
    return jax.shard_map(
        body,
        mesh=fine,
        in_specs=(spec, spec, spec, P(), P()),
        out_specs=spec,
        check_vma=False,
    )
```

```python
import jax
import jax.numpy as jnp
from jax import lax
from jax.experimental import pallas as pl
from jax.experimental.pallas import tpu as pltpu
from jax.sharding import PartitionSpec as P

HEAD = 128
LOG2E = 1.4426950408889634
BLOCK_Q = 384
KEY_STEP = 256
REACH = 5
CORES = 2


def pack(queries, keys, values, slots):
    _, tokens, width = queries.shape
    parts = 4
    here = width // parts

    def kernel(q_ref, k_ref, v_ref, o_ref):
        for i, ref in enumerate((q_ref, k_ref, v_ref)):
            for h in range(here // HEAD):
                o_ref[h, i] = ref[0, :, h * HEAD : (h + 1) * HEAD]

    return pl.pallas_call(
        kernel,
        grid=(parts,),
        out_shape=jax.ShapeDtypeStruct((slots, 3, tokens, HEAD), queries.dtype),
        in_specs=[pl.BlockSpec((1, tokens, here), lambda g: (0, 0, g))] * 3,
        out_specs=pl.BlockSpec((here // HEAD, 3, tokens, HEAD), lambda g: (g, 0, 0, 0)),
        compiler_params=pltpu.CompilerParams(vmem_limit_bytes=32 * 2**20),
        name="pack",
    )(queries, keys, values)


def attend(lengths, span_mask, place, got, other_keys, other_values):
    groups = span_mask.shape[0]
    run = got.shape[2]
    runs = got.shape[0] // groups
    rows = runs * run
    span = CORES * rows
    sizes = [n for n in range(KEY_STEP, span + 1, KEY_STEP) if n >= span // 2]

    def kernel(len_ref, mask_ref, place_ref, got_ref, other_k_ref, other_v_ref, o_ref, q_in, keys, values, ones, q, top, acc, sems):
        core = place_ref[1]
        by_run = (groups, runs, CORES, run, HEAD)
        keys_by_run, values_by_run = keys.reshape(by_run), values.reshape(by_run)

        def copies(c):
            here = pl.ds(c * runs, runs)
            pairs = (
                (got_ref.at[here, 0], q_in.at[c]),
                (got_ref.at[here, 1], keys_by_run.at[c, :, core]),
                (got_ref.at[here, 2], values_by_run.at[c, :, core]),
                (other_k_ref.at[here], keys_by_run.at[c, :, 1 - core]),
                (other_v_ref.at[here], values_by_run.at[c, :, 1 - core]),
            )
            return [pltpu.make_async_copy(src, dst, sems.at[c, i]) for i, (src, dst) in enumerate(pairs)]

        def start(c, carry):
            for copy in copies(c):
                copy.start()
            return carry

        def clean(c):
            count = len_ref[c]
            base = (count - 1) // KEY_STEP * KEY_STEP
            here = pl.ds(pl.multiple_of(c * span + base, KEY_STEP), KEY_STEP)
            live = (base + lax.broadcasted_iota(jnp.int32, (KEY_STEP, HEAD), 0)) < count
            first = keys[pl.ds(pl.multiple_of(c * span, KEY_STEP), 16), :][0:1]
            keys[here, :] = jnp.where(live, keys[here, :], first)
            values[here, :] = jnp.where(live, values[here, :], jnp.bfloat16(0))
            ones[here, :] = jnp.where(live, jnp.bfloat16(1), jnp.bfloat16(0))

        def step(c, n, fresh):
            here = pl.ds(pl.multiple_of(c * span, KEY_STEP), n)
            k = keys[here, :]
            k = jnp.concatenate([k, k], axis=1)
            v = jnp.concatenate([values[here, :], ones[here, :]], axis=1)

            def scores(i):
                return lax.dot_general(
                    q[i * BLOCK_Q : (i + 1) * BLOCK_Q, :],
                    k,
                    (((1,), (1,)), ((), ())),
                    preferred_element_type=jnp.float32,
                )

            later = scores(0)
            for i in range(rows // BLOCK_Q):
                block = slice(i * BLOCK_Q, (i + 1) * BLOCK_Q)
                score = later
                if i + 1 < rows // BLOCK_Q:
                    later = scores(i + 1)
                new_top = jnp.max(score, axis=1, keepdims=True)
                if not fresh:
                    old_top = top[block, 0:1]
                    new_top = jnp.maximum(old_top, new_top)
                weight = jnp.exp2(score - new_top).astype(jnp.bfloat16)
                update = jnp.dot(weight, v, preferred_element_type=jnp.float32)
                if fresh:
                    acc[block, :] = update
                else:
                    acc[block, :] = acc[block, :] * jnp.exp2(old_top - new_top) + update
                top[block, :] = jnp.broadcast_to(new_top, (BLOCK_Q, HEAD))

        def by_length(c, fresh):
            steps = (len_ref[c] + KEY_STEP - 1) // KEY_STEP
            for n in sizes:
                pl.when(steps == n // KEY_STEP)(lambda n=n: step(c, n, fresh))

        def one_group(s, carry):
            for copy in copies(s):
                copy.wait()
            clean(s)
            scaled = q_in[s].reshape(rows, HEAD).astype(jnp.float32) * (LOG2E * HEAD**-0.5)
            high = scaled.astype(jnp.bfloat16)
            q[:, :HEAD] = high
            q[:, HEAD:] = (scaled - high.astype(jnp.float32)).astype(jnp.bfloat16)
            by_length(s, True)

            def earlier(c, inner):
                pl.when(mask_ref[s, c] > 0)(lambda: by_length(c, False))
                return inner

            lax.fori_loop(jnp.maximum(s - (REACH - 1), 0), s, earlier, 0)
            total = acc[...]
            o_ref[lax.rem(s + 1, groups)] = (total[:, :HEAD] / total[:, HEAD:]).astype(jnp.bfloat16)
            return carry

        @pl.when(place_ref[0] > 0)
        def _():
            lax.fori_loop(0, groups, start, 0)
            ones[...] = jnp.ones(ones.shape, jnp.bfloat16)
            lax.fori_loop(0, groups, one_group, 0)

    smem = pl.BlockSpec(memory_space=pltpu.SMEM)
    where_it_is = pl.BlockSpec(memory_space=pl.ANY)
    bf16, f32 = jnp.bfloat16, jnp.float32
    return pl.pallas_call(
        kernel,
        out_shape=jax.ShapeDtypeStruct((groups, rows, HEAD), bf16),
        in_specs=[smem] * 3 + [where_it_is] * 3,
        out_specs=pl.BlockSpec(memory_space=pltpu.VMEM),
        scratch_shapes=[
            pltpu.VMEM((groups, runs, run, HEAD), bf16),
            pltpu.VMEM((groups * span, HEAD), bf16),
            pltpu.VMEM((groups * span, HEAD), bf16),
            pltpu.VMEM((groups * span, HEAD), bf16),
            pltpu.VMEM((rows, 2 * HEAD), bf16),
            pltpu.VMEM((rows, HEAD), f32),
            pltpu.VMEM((rows, 2 * HEAD), f32),
            pltpu.SemaphoreType.DMA((groups, 5)),
        ],
        compiler_params=pltpu.CompilerParams(vmem_limit_bytes=48 * 2**20),
        name="attend",
    )(lengths, span_mask, place, got, other_keys, other_values)


CHIPS = ("xh", "z", "xl", "y")


def body(queries, keys, values, lengths, span_mask):
    tokens, width = queries.shape[1:]
    heads = width // HEAD
    chips = lax.axis_size(CHIPS)
    core = lax.axis_index("core")

    sent = pack(queries, keys, values, chips)
    got = lax.all_to_all(sent, CHIPS, 0, 0, tiled=True)

    rest, own_keys = lax.optimization_barrier((got, got[:, 1]))
    other_keys = lax.ppermute(own_keys, "core", [(0, 1), (1, 0)])
    other_values = lax.ppermute(rest[:, 2], "core", [(0, 1), (1, 0)])
    active = (lax.axis_index(CHIPS) < heads).astype(jnp.int32)
    out = attend(lengths, span_mask, jnp.stack([active, core]), got, other_keys, other_values)
    back = lax.all_to_all(out.reshape(chips, tokens, HEAD), CHIPS, 0, 0, tiled=True)[:heads]
    return jnp.transpose(back, (1, 0, 2)).reshape(1, tokens, width)


def solution(mesh):
    fine = jax.sharding.Mesh(mesh.devices.reshape(2, 4, 2, 4, 2), ("xh", "z", "xl", "y", "core"))
    spec = P(("xh", "z"), ("xl", "y", "core"), None)
    return jax.shard_map(
        body,
        mesh=fine,
        in_specs=(spec, spec, spec, P(), P()),
        out_specs=spec,
        check_vma=False,
    )
```

```python
import jax
import jax.numpy as jnp
from jax import lax
from jax.experimental import pallas as pl
from jax.experimental.pallas import tpu as pltpu
from jax.sharding import PartitionSpec as P

HEAD = 128
LOG2E = 1.4426950408889634
BLOCK_Q = 384
KEY_STEP = 256
REACH = 5
CORES = 2


def pack(queries, keys, values, slots):
    _, tokens, width = queries.shape
    parts = 4
    here = width // parts
    heads = here // HEAD

    def kernel(q_ref, k_ref, v_ref, o_ref, held, ready, in_sems, out_sems):
        def load(g, i):
            columns = slice(g * here, (g + 1) * here)
            return pltpu.make_async_copy((q_ref, k_ref, v_ref)[i].at[0, :, columns], held.at[g, i], in_sems.at[g, i])

        def store(g):
            return pltpu.make_async_copy(ready.at[g], o_ref.at[pl.ds(g * heads, heads)], out_sems.at[g])

        for g in range(parts):
            for i in range(3):
                load(g, i).start()
        for g in range(parts):
            for i in range(3):
                load(g, i).wait()
                for h in range(heads):
                    ready[g, h, i] = held[g, i, :, h * HEAD : (h + 1) * HEAD]
            store(g).start()
        for g in range(parts):
            store(g).wait()

    return pl.pallas_call(
        kernel,
        out_shape=jax.ShapeDtypeStruct((slots, 3, tokens, HEAD), queries.dtype),
        in_specs=[pl.BlockSpec(memory_space=pl.ANY)] * 3,
        out_specs=pl.BlockSpec(memory_space=pl.ANY),
        scratch_shapes=[
            pltpu.VMEM((parts, 3, tokens, here), queries.dtype),
            pltpu.VMEM((parts, heads, 3, tokens, HEAD), queries.dtype),
            pltpu.SemaphoreType.DMA((parts, 3)),
            pltpu.SemaphoreType.DMA((parts,)),
        ],
        compiler_params=pltpu.CompilerParams(vmem_limit_bytes=56 * 2**20),
        name="pack",
    )(queries, keys, values)


def attend(lengths, span_mask, place, got, other):
    groups = span_mask.shape[0]
    run = got.shape[2]
    runs = got.shape[0] // groups
    rows = runs * run
    span = CORES * rows
    sizes = [n for n in range(KEY_STEP, span + 1, KEY_STEP) if n >= span // 2]

    def kernel(len_ref, mask_ref, place_ref, got_ref, other_ref, o_ref, q_in, keys, values, ones, q, top, acc, sems):
        core = place_ref[1]
        by_run = (groups, runs, CORES, run, HEAD)
        keys_by_run, values_by_run = keys.reshape(by_run), values.reshape(by_run)

        def copies(c):
            here = pl.ds(c * runs, runs)
            pairs = (
                (got_ref.at[here, 0], q_in.at[c]),
                (got_ref.at[here, 1], keys_by_run.at[c, :, core]),
                (got_ref.at[here, 2], values_by_run.at[c, :, core]),
                (other_ref.at[here, 0], keys_by_run.at[c, :, 1 - core]),
                (other_ref.at[here, 1], values_by_run.at[c, :, 1 - core]),
            )
            return [pltpu.make_async_copy(src, dst, sems.at[c, i]) for i, (src, dst) in enumerate(pairs)]

        def start(c, carry):
            for copy in copies(c):
                copy.start()
            return carry

        def clean(c):
            count = len_ref[c]
            base = (count - 1) // KEY_STEP * KEY_STEP
            here = pl.ds(pl.multiple_of(c * span + base, KEY_STEP), KEY_STEP)
            live = (base + lax.broadcasted_iota(jnp.int32, (KEY_STEP, HEAD), 0)) < count
            first = keys[pl.ds(pl.multiple_of(c * span, KEY_STEP), 16), :][0:1]
            keys[here, :] = jnp.where(live, keys[here, :], first)
            values[here, :] = jnp.where(live, values[here, :], jnp.bfloat16(0))
            ones[here, :] = jnp.where(live, jnp.bfloat16(1), jnp.bfloat16(0))

        def step(c, n, fresh):
            here = pl.ds(pl.multiple_of(c * span, KEY_STEP), n)
            k = keys[here, :]
            k = jnp.concatenate([k, k], axis=1)
            v = jnp.concatenate([values[here, :], ones[here, :]], axis=1)

            def scores(i):
                return lax.dot_general(
                    q[i * BLOCK_Q : (i + 1) * BLOCK_Q, :],
                    k,
                    (((1,), (1,)), ((), ())),
                    preferred_element_type=jnp.float32,
                )

            later = scores(0)
            for i in range(rows // BLOCK_Q):
                block = slice(i * BLOCK_Q, (i + 1) * BLOCK_Q)
                score = later
                if i + 1 < rows // BLOCK_Q:
                    later = scores(i + 1)
                new_top = jnp.max(score, axis=1, keepdims=True)
                if not fresh:
                    old_top = top[block, 0:1]
                    new_top = jnp.maximum(old_top, new_top)
                weight = jnp.exp2(score - new_top).astype(jnp.bfloat16)
                update = jnp.dot(weight, v, preferred_element_type=jnp.float32)
                if fresh:
                    acc[block, :] = update
                else:
                    acc[block, :] = acc[block, :] * jnp.exp2(old_top - new_top) + update
                top[block, :] = jnp.broadcast_to(new_top, (BLOCK_Q, HEAD))

        def by_length(c, fresh):
            steps = (len_ref[c] + KEY_STEP - 1) // KEY_STEP
            for n in sizes:
                pl.when(steps == n // KEY_STEP)(lambda n=n: step(c, n, fresh))

        def one_group(s, carry):
            for copy in copies(s):
                copy.wait()
            clean(s)
            scaled = q_in[s].reshape(rows, HEAD).astype(jnp.float32) * (LOG2E * HEAD**-0.5)
            high = scaled.astype(jnp.bfloat16)
            q[:, :HEAD] = high
            q[:, HEAD:] = (scaled - high.astype(jnp.float32)).astype(jnp.bfloat16)
            by_length(s, True)

            def earlier(c, inner):
                pl.when(mask_ref[s, c] > 0)(lambda: by_length(c, False))
                return inner

            lax.fori_loop(jnp.maximum(s - (REACH - 1), 0), s, earlier, 0)
            total = acc[...]
            o_ref[lax.rem(s + 1, groups)] = (total[:, :HEAD] / total[:, HEAD:]).astype(jnp.bfloat16)
            return carry

        @pl.when(place_ref[0] > 0)
        def _():
            lax.fori_loop(0, groups, start, 0)
            ones[...] = jnp.ones(ones.shape, jnp.bfloat16)
            lax.fori_loop(0, groups, one_group, 0)

    smem = pl.BlockSpec(memory_space=pltpu.SMEM)
    where_it_is = pl.BlockSpec(memory_space=pl.ANY)
    bf16, f32 = jnp.bfloat16, jnp.float32
    return pl.pallas_call(
        kernel,
        out_shape=jax.ShapeDtypeStruct((groups, rows, HEAD), bf16),
        in_specs=[smem] * 3 + [where_it_is] * 2,
        out_specs=pl.BlockSpec(memory_space=pltpu.VMEM),
        scratch_shapes=[
            pltpu.VMEM((groups, runs, run, HEAD), bf16),
            pltpu.VMEM((groups * span, HEAD), bf16),
            pltpu.VMEM((groups * span, HEAD), bf16),
            pltpu.VMEM((groups * span, HEAD), bf16),
            pltpu.VMEM((rows, 2 * HEAD), bf16),
            pltpu.VMEM((rows, HEAD), f32),
            pltpu.VMEM((rows, 2 * HEAD), f32),
            pltpu.SemaphoreType.DMA((groups, 5)),
        ],
        compiler_params=pltpu.CompilerParams(vmem_limit_bytes=48 * 2**20),
        name="attend",
    )(lengths, span_mask, place, got, other)


CHIPS = ("xh", "z", "xl", "y")


def body(queries, keys, values, lengths, span_mask):
    tokens, width = queries.shape[1:]
    heads = width // HEAD
    chips = lax.axis_size(CHIPS)
    core = lax.axis_index("core")

    sent = pack(queries, keys, values, chips)
    got = lax.all_to_all(sent, CHIPS, 0, 0, tiled=True)

    other = lax.ppermute(got[:, 1:], "core", [(0, 1), (1, 0)])
    active = (lax.axis_index(CHIPS) < heads).astype(jnp.int32)
    out = attend(lengths, span_mask, jnp.stack([active, core]), got, other)
    back = lax.all_to_all(out.reshape(chips, tokens, HEAD), CHIPS, 0, 0, tiled=True)[:heads]
    return jnp.transpose(back, (1, 0, 2)).reshape(1, tokens, width)


def solution(mesh):
    fine = jax.sharding.Mesh(mesh.devices.reshape(2, 4, 2, 4, 2), ("xh", "z", "xl", "y", "core"))
    spec = P(("xh", "z"), ("xl", "y", "core"), None)
    return jax.shard_map(
        body,
        mesh=fine,
        in_specs=(spec, spec, spec, P(), P()),
        out_specs=spec,
        check_vma=False,
    )
```

```python
import jax
import jax.numpy as jnp
from jax import lax
from jax.experimental import pallas as pl
from jax.experimental.pallas import tpu as pltpu
from jax.sharding import PartitionSpec as P

HEAD = 128
LOG2E = 1.4426950408889634
BLOCK_Q = 384
KEY_STEP = 256
REACH = 5
CORES = 2
WEIGHT_LIMIT = 2.0**60
FIRST, KEEP, MOVE = range(3)


def fold(weight):
    best = weight[:, :HEAD]
    for j in range(HEAD, weight.shape[1], HEAD):
        best = jnp.maximum(best, weight[:, j : j + HEAD])
    while best.shape[0] % 32 == 0:
        half = best.shape[0] // 2
        best = jnp.maximum(best[:half], best[half:])
    tile = best[:16]
    for j in range(16, best.shape[0], 16):
        tile = jnp.maximum(tile, best[j : j + 16])
    return tile


def pack(queries, keys, values, slots):
    _, tokens, width = queries.shape
    parts = 4
    here = width // parts
    heads = here // HEAD

    def kernel(q_ref, k_ref, v_ref, o_ref, held, ready, in_sems, out_sems):
        def load(g, i):
            columns = slice(g * here, (g + 1) * here)
            return pltpu.make_async_copy((q_ref, k_ref, v_ref)[i].at[0, :, columns], held.at[g, i], in_sems.at[g, i])

        def store(g):
            return pltpu.make_async_copy(ready.at[g], o_ref.at[pl.ds(g * heads, heads)], out_sems.at[g])

        for g in range(parts):
            for i in range(3):
                load(g, i).start()
        for g in range(parts):
            for i in range(3):
                load(g, i).wait()
                for h in range(heads):
                    ready[g, h, i] = held[g, i, :, h * HEAD : (h + 1) * HEAD]
            store(g).start()
        for g in range(parts):
            store(g).wait()

    return pl.pallas_call(
        kernel,
        out_shape=jax.ShapeDtypeStruct((slots, 3, tokens, HEAD), queries.dtype),
        in_specs=[pl.BlockSpec(memory_space=pl.ANY)] * 3,
        out_specs=pl.BlockSpec(memory_space=pl.ANY),
        scratch_shapes=[
            pltpu.VMEM((parts, 3, tokens, here), queries.dtype),
            pltpu.VMEM((parts, heads, 3, tokens, HEAD), queries.dtype),
            pltpu.SemaphoreType.DMA((parts, 3)),
            pltpu.SemaphoreType.DMA((parts,)),
        ],
        compiler_params=pltpu.CompilerParams(vmem_limit_bytes=56 * 2**20),
        name="pack",
    )(queries, keys, values)


def attend(lengths, span_mask, place, got, other):
    groups = span_mask.shape[0]
    run = got.shape[2]
    runs = got.shape[0] // groups
    rows = runs * run
    span = CORES * rows
    sizes = [n for n in range(KEY_STEP, span + 1, KEY_STEP) if n >= span // 2]

    def kernel(len_ref, mask_ref, place_ref, got_ref, other_ref, o_ref, q_in, keys, values, ones, q, top, acc, largest, sems):
        core = place_ref[1]
        by_run = (groups, runs, CORES, run, HEAD)
        keys_by_run, values_by_run = keys.reshape(by_run), values.reshape(by_run)

        def copies(c):
            here = pl.ds(c * runs, runs)
            pairs = (
                (got_ref.at[here, 0], q_in.at[c]),
                (got_ref.at[here, 1], keys_by_run.at[c, :, core]),
                (got_ref.at[here, 2], values_by_run.at[c, :, core]),
                (other_ref.at[here, 0], keys_by_run.at[c, :, 1 - core]),
                (other_ref.at[here, 1], values_by_run.at[c, :, 1 - core]),
            )
            return [pltpu.make_async_copy(src, dst, sems.at[c, i]) for i, (src, dst) in enumerate(pairs)]

        def start(c, carry):
            for copy in copies(c):
                copy.start()
            return carry

        def clean(c):
            count = len_ref[c]
            base = (count - 1) // KEY_STEP * KEY_STEP
            here = pl.ds(pl.multiple_of(c * span + base, KEY_STEP), KEY_STEP)
            live = (base + lax.broadcasted_iota(jnp.int32, (KEY_STEP, HEAD), 0)) < count
            first = keys[pl.ds(pl.multiple_of(c * span, KEY_STEP), 16), :][0:1]
            keys[here, :] = jnp.where(live, keys[here, :], first)
            values[here, :] = jnp.where(live, values[here, :], jnp.bfloat16(0))
            ones[here, :] = jnp.where(live, jnp.bfloat16(1), jnp.bfloat16(0))

        def step(c, n, kind):
            here = pl.ds(pl.multiple_of(c * span, KEY_STEP), n)
            k = keys[here, :]
            k = jnp.concatenate([k, k], axis=1)
            v = jnp.concatenate([values[here, :], ones[here, :]], axis=1)

            def scores(i):
                return lax.dot_general(
                    q[i * BLOCK_Q : (i + 1) * BLOCK_Q, :],
                    k,
                    (((1,), (1,)), ((), ())),
                    preferred_element_type=jnp.float32,
                )

            later = scores(0)
            for i in range(rows // BLOCK_Q):
                block = slice(i * BLOCK_Q, (i + 1) * BLOCK_Q)
                score = later
                if i + 1 < rows // BLOCK_Q:
                    later = scores(i + 1)
                if kind == KEEP:
                    kept = jnp.concatenate([top[block, :]] * (n // HEAD), axis=1)
                    weight = jnp.exp2(score - kept).astype(jnp.bfloat16)
                    largest[...] = jnp.maximum(largest[...], fold(weight))
                    acc[block, :] += jnp.dot(weight, v, preferred_element_type=jnp.float32)
                    continue
                new_top = jnp.max(score, axis=1, keepdims=True)
                if kind == MOVE:
                    old_top = top[block, 0:1]
                    new_top = jnp.maximum(old_top, new_top)
                weight = jnp.exp2(score - new_top).astype(jnp.bfloat16)
                update = jnp.dot(weight, v, preferred_element_type=jnp.float32)
                if kind == FIRST:
                    acc[block, :] = update
                else:
                    acc[block, :] = acc[block, :] * jnp.exp2(old_top - new_top) + update
                top[block, :] = jnp.broadcast_to(new_top, (BLOCK_Q, HEAD))

        def by_length(c, kind):
            steps = (len_ref[c] + KEY_STEP - 1) // KEY_STEP
            for n in sizes:
                pl.when(steps == n // KEY_STEP)(lambda n=n: step(c, n, kind))

        def one_group(s, carry):
            for copy in copies(s):
                copy.wait()
            clean(s)
            scaled = q_in[s].reshape(rows, HEAD).astype(jnp.float32) * (LOG2E * HEAD**-0.5)
            high = scaled.astype(jnp.bfloat16)
            q[:, :HEAD] = high
            q[:, HEAD:] = (scaled - high.astype(jnp.float32)).astype(jnp.bfloat16)

            def attempt(state):
                again, _ = state
                by_length(s, FIRST)
                largest[...] = jnp.zeros(largest.shape, jnp.bfloat16)

                def earlier(c, inner):
                    live = mask_ref[s, c] > 0
                    pl.when(live & (again == 0))(lambda: by_length(c, KEEP))
                    pl.when(live & (again > 0))(lambda: by_length(c, MOVE))
                    return inner

                lax.fori_loop(jnp.maximum(s - (REACH - 1), 0), s, earlier, 0)
                over = jnp.max(largest[...].astype(jnp.float32)) > WEIGHT_LIMIT
                return again + 1, over.astype(jnp.int32)

            zero = jnp.int32(0)
            lax.while_loop(lambda x: (x[0] == 0) | ((x[0] == 1) & (x[1] > 0)), attempt, (zero, zero))
            total = acc[...]
            o_ref[lax.rem(s + 1, groups)] = (total[:, :HEAD] / total[:, HEAD:]).astype(jnp.bfloat16)
            return carry

        @pl.when(place_ref[0] > 0)
        def _():
            lax.fori_loop(0, groups, start, 0)
            ones[...] = jnp.ones(ones.shape, jnp.bfloat16)
            lax.fori_loop(0, groups, one_group, 0)

    smem = pl.BlockSpec(memory_space=pltpu.SMEM)
    where_it_is = pl.BlockSpec(memory_space=pl.ANY)
    bf16, f32 = jnp.bfloat16, jnp.float32
    return pl.pallas_call(
        kernel,
        out_shape=jax.ShapeDtypeStruct((groups, rows, HEAD), bf16),
        in_specs=[smem] * 3 + [where_it_is] * 2,
        out_specs=pl.BlockSpec(memory_space=pltpu.VMEM),
        scratch_shapes=[
            pltpu.VMEM((groups, runs, run, HEAD), bf16),
            pltpu.VMEM((groups * span, HEAD), bf16),
            pltpu.VMEM((groups * span, HEAD), bf16),
            pltpu.VMEM((groups * span, HEAD), bf16),
            pltpu.VMEM((rows, 2 * HEAD), bf16),
            pltpu.VMEM((rows, HEAD), f32),
            pltpu.VMEM((rows, 2 * HEAD), f32),
            pltpu.VMEM((16, HEAD), bf16),
            pltpu.SemaphoreType.DMA((groups, 5)),
        ],
        compiler_params=pltpu.CompilerParams(vmem_limit_bytes=48 * 2**20),
        name="attend",
    )(lengths, span_mask, place, got, other)


CHIPS = ("xh", "z", "xl", "y")


def body(queries, keys, values, lengths, span_mask):
    tokens, width = queries.shape[1:]
    heads = width // HEAD
    chips = lax.axis_size(CHIPS)
    core = lax.axis_index("core")

    sent = pack(queries, keys, values, chips)
    got = lax.all_to_all(sent, CHIPS, 0, 0, tiled=True)

    other = lax.ppermute(got[:, 1:], "core", [(0, 1), (1, 0)])
    active = (lax.axis_index(CHIPS) < heads).astype(jnp.int32)
    out = attend(lengths, span_mask, jnp.stack([active, core]), got, other)
    back = lax.all_to_all(out.reshape(chips, tokens, HEAD), CHIPS, 0, 0, tiled=True)[:heads]
    return jnp.transpose(back, (1, 0, 2)).reshape(1, tokens, width)


def solution(mesh):
    fine = jax.sharding.Mesh(mesh.devices.reshape(2, 4, 2, 4, 2), ("xh", "z", "xl", "y", "core"))
    spec = P(("xh", "z"), ("xl", "y", "core"), None)
    return jax.shard_map(
        body,
        mesh=fine,
        in_specs=(spec, spec, spec, P(), P()),
        out_specs=spec,
        check_vma=False,
    )
```

```python
import jax
import jax.numpy as jnp
from jax import lax
from jax.experimental import pallas as pl
from jax.experimental.pallas import tpu as pltpu
from jax.sharding import PartitionSpec as P

HEAD = 128
LOG2E = 1.4426950408889634
BLOCK_Q = 384
KEY_STEP = 256
REACH = 5
CORES = 2
WEIGHT_LIMIT = 2.0**60
FIRST, KEEP, MOVE = range(3)


def fold(weight):
    best = weight[:, :HEAD]
    for j in range(HEAD, weight.shape[1], HEAD):
        best = jnp.maximum(best, weight[:, j : j + HEAD])
    while best.shape[0] % 32 == 0:
        half = best.shape[0] // 2
        best = jnp.maximum(best[:half], best[half:])
    tile = best[:16]
    for j in range(16, best.shape[0], 16):
        tile = jnp.maximum(tile, best[j : j + 16])
    return tile


def pack(queries, keys, values, slots):
    _, tokens, width = queries.shape
    parts = 4
    here = width // parts
    heads = here // HEAD

    def kernel(q_ref, k_ref, v_ref, o_ref, held, ready, in_sems, out_sems):
        def load(g, i):
            columns = slice(g * here, (g + 1) * here)
            return pltpu.make_async_copy((q_ref, k_ref, v_ref)[i].at[0, :, columns], held.at[g, i], in_sems.at[g, i])

        def store(g):
            return pltpu.make_async_copy(ready.at[g], o_ref.at[pl.ds(g * heads, heads)], out_sems.at[g])

        for g in range(parts):
            for i in range(3):
                load(g, i).start()
        for g in range(parts):
            for i in range(3):
                load(g, i).wait()
                for h in range(heads):
                    ready[g, h, i] = held[g, i, :, h * HEAD : (h + 1) * HEAD]
            store(g).start()
        for g in range(parts):
            store(g).wait()

    return pl.pallas_call(
        kernel,
        out_shape=jax.ShapeDtypeStruct((slots, 3, tokens, HEAD), queries.dtype),
        in_specs=[pl.BlockSpec(memory_space=pl.ANY)] * 3,
        out_specs=pl.BlockSpec(memory_space=pl.ANY),
        scratch_shapes=[
            pltpu.VMEM((parts, 3, tokens, here), queries.dtype),
            pltpu.VMEM((parts, heads, 3, tokens, HEAD), queries.dtype),
            pltpu.SemaphoreType.DMA((parts, 3)),
            pltpu.SemaphoreType.DMA((parts,)),
        ],
        compiler_params=pltpu.CompilerParams(vmem_limit_bytes=56 * 2**20),
        name="pack",
    )(queries, keys, values)


def unpack(back, heads):
    _, tokens, _ = back.shape

    def kernel(back_ref, o_ref, sems):
        copies = [
            pltpu.make_async_copy(back_ref.at[h], o_ref.at[0, :, h * HEAD : (h + 1) * HEAD], sems.at[h])
            for h in range(heads)
        ]
        for copy in copies:
            copy.start()
        for copy in copies:
            copy.wait()

    return pl.pallas_call(
        kernel,
        out_shape=jax.ShapeDtypeStruct((1, tokens, heads * HEAD), back.dtype),
        in_specs=[pl.BlockSpec(memory_space=pl.ANY)],
        out_specs=pl.BlockSpec(memory_space=pl.ANY),
        scratch_shapes=[pltpu.SemaphoreType.DMA((heads,))],
        compiler_params=pltpu.CompilerParams(vmem_limit_bytes=16 * 2**20),
        name="unpack",
    )(back)


def attend(lengths, span_mask, place, got, other):
    groups = span_mask.shape[0]
    run = got.shape[2]
    runs = got.shape[0] // groups
    rows = runs * run
    span = CORES * rows
    sizes = [n for n in range(KEY_STEP, span + 1, KEY_STEP) if n >= span // 2]

    def kernel(len_ref, mask_ref, place_ref, got_ref, other_ref, o_ref, q_in, keys, values, ones, q, top, acc, largest, sems):
        core = place_ref[1]
        by_run = (groups, runs, CORES, run, HEAD)
        keys_by_run, values_by_run = keys.reshape(by_run), values.reshape(by_run)

        def copies(c):
            here = pl.ds(c * runs, runs)
            pairs = (
                (got_ref.at[here, 0], q_in.at[c]),
                (got_ref.at[here, 1], keys_by_run.at[c, :, core]),
                (got_ref.at[here, 2], values_by_run.at[c, :, core]),
                (other_ref.at[here, 0], keys_by_run.at[c, :, 1 - core]),
                (other_ref.at[here, 1], values_by_run.at[c, :, 1 - core]),
            )
            return [pltpu.make_async_copy(src, dst, sems.at[c, i]) for i, (src, dst) in enumerate(pairs)]

        def start(c, carry):
            for copy in copies(c):
                copy.start()
            return carry

        def clean(c):
            count = len_ref[c]
            base = (count - 1) // KEY_STEP * KEY_STEP
            here = pl.ds(pl.multiple_of(c * span + base, KEY_STEP), KEY_STEP)
            live = (base + lax.broadcasted_iota(jnp.int32, (KEY_STEP, HEAD), 0)) < count
            first = keys[pl.ds(pl.multiple_of(c * span, KEY_STEP), 16), :][0:1]
            keys[here, :] = jnp.where(live, keys[here, :], first)
            values[here, :] = jnp.where(live, values[here, :], jnp.bfloat16(0))
            ones[here, :] = jnp.where(live, jnp.bfloat16(1), jnp.bfloat16(0))

        def step(c, n, kind):
            here = pl.ds(pl.multiple_of(c * span, KEY_STEP), n)
            k = keys[here, :]
            k = jnp.concatenate([k, k], axis=1)
            v = jnp.concatenate([values[here, :], ones[here, :]], axis=1)

            def scores(i):
                return lax.dot_general(
                    q[i * BLOCK_Q : (i + 1) * BLOCK_Q, :],
                    k,
                    (((1,), (1,)), ((), ())),
                    preferred_element_type=jnp.float32,
                )

            later = scores(0)
            for i in range(rows // BLOCK_Q):
                block = slice(i * BLOCK_Q, (i + 1) * BLOCK_Q)
                score = later
                if i + 1 < rows // BLOCK_Q:
                    later = scores(i + 1)
                if kind == KEEP:
                    kept = jnp.concatenate([top[block, :]] * (n // HEAD), axis=1)
                    weight = jnp.exp2(score - kept).astype(jnp.bfloat16)
                    largest[...] = jnp.maximum(largest[...], fold(weight))
                    acc[block, :] += jnp.dot(weight, v, preferred_element_type=jnp.float32)
                    continue
                new_top = jnp.max(score, axis=1, keepdims=True)
                if kind == MOVE:
                    old_top = top[block, 0:1]
                    new_top = jnp.maximum(old_top, new_top)
                weight = jnp.exp2(score - new_top).astype(jnp.bfloat16)
                update = jnp.dot(weight, v, preferred_element_type=jnp.float32)
                if kind == FIRST:
                    acc[block, :] = update
                else:
                    acc[block, :] = acc[block, :] * jnp.exp2(old_top - new_top) + update
                top[block, :] = jnp.broadcast_to(new_top, (BLOCK_Q, HEAD))

        def by_length(c, kind):
            steps = (len_ref[c] + KEY_STEP - 1) // KEY_STEP
            for n in sizes:
                pl.when(steps == n // KEY_STEP)(lambda n=n: step(c, n, kind))

        def one_group(s, carry):
            for copy in copies(s):
                copy.wait()
            clean(s)
            scaled = q_in[s].reshape(rows, HEAD).astype(jnp.float32) * (LOG2E * HEAD**-0.5)
            high = scaled.astype(jnp.bfloat16)
            q[:, :HEAD] = high
            q[:, HEAD:] = (scaled - high.astype(jnp.float32)).astype(jnp.bfloat16)

            def attempt(state):
                again, _ = state
                by_length(s, FIRST)
                largest[...] = jnp.zeros(largest.shape, jnp.bfloat16)

                def earlier(c, inner):
                    live = mask_ref[s, c] > 0
                    pl.when(live & (again == 0))(lambda: by_length(c, KEEP))
                    pl.when(live & (again > 0))(lambda: by_length(c, MOVE))
                    return inner

                lax.fori_loop(jnp.maximum(s - (REACH - 1), 0), s, earlier, 0)
                over = jnp.max(largest[...].astype(jnp.float32)) > WEIGHT_LIMIT
                return again + 1, over.astype(jnp.int32)

            zero = jnp.int32(0)
            lax.while_loop(lambda x: (x[0] == 0) | ((x[0] == 1) & (x[1] > 0)), attempt, (zero, zero))
            total = acc[...]
            o_ref[lax.rem(s + 1, groups)] = (total[:, :HEAD] / total[:, HEAD:]).astype(jnp.bfloat16)
            return carry

        @pl.when(place_ref[0] > 0)
        def _():
            lax.fori_loop(0, groups, start, 0)
            ones[...] = jnp.ones(ones.shape, jnp.bfloat16)
            lax.fori_loop(0, groups, one_group, 0)

    smem = pl.BlockSpec(memory_space=pltpu.SMEM)
    where_it_is = pl.BlockSpec(memory_space=pl.ANY)
    bf16, f32 = jnp.bfloat16, jnp.float32
    return pl.pallas_call(
        kernel,
        out_shape=jax.ShapeDtypeStruct((groups, rows, HEAD), bf16),
        in_specs=[smem] * 3 + [where_it_is] * 2,
        out_specs=pl.BlockSpec(memory_space=pltpu.VMEM),
        scratch_shapes=[
            pltpu.VMEM((groups, runs, run, HEAD), bf16),
            pltpu.VMEM((groups * span, HEAD), bf16),
            pltpu.VMEM((groups * span, HEAD), bf16),
            pltpu.VMEM((groups * span, HEAD), bf16),
            pltpu.VMEM((rows, 2 * HEAD), bf16),
            pltpu.VMEM((rows, HEAD), f32),
            pltpu.VMEM((rows, 2 * HEAD), f32),
            pltpu.VMEM((16, HEAD), bf16),
            pltpu.SemaphoreType.DMA((groups, 5)),
        ],
        compiler_params=pltpu.CompilerParams(vmem_limit_bytes=48 * 2**20),
        name="attend",
    )(lengths, span_mask, place, got, other)


CHIPS = ("xh", "z", "xl", "y")


def body(queries, keys, values, lengths, span_mask):
    tokens, width = queries.shape[1:]
    heads = width // HEAD
    chips = lax.axis_size(CHIPS)
    core = lax.axis_index("core")

    sent = pack(queries, keys, values, chips)
    got = lax.all_to_all(sent, CHIPS, 0, 0, tiled=True)

    other = lax.ppermute(got[:, 1:], "core", [(0, 1), (1, 0)])
    active = (lax.axis_index(CHIPS) < heads).astype(jnp.int32)
    out = attend(lengths, span_mask, jnp.stack([active, core]), got, other)
    back = lax.all_to_all(out.reshape(chips, tokens, HEAD), CHIPS, 0, 0, tiled=True)
    return unpack(back, heads)


def solution(mesh):
    fine = jax.sharding.Mesh(mesh.devices.reshape(2, 4, 2, 4, 2), ("xh", "z", "xl", "y", "core"))
    spec = P(("xh", "z"), ("xl", "y", "core"), None)
    return jax.shard_map(
        body,
        mesh=fine,
        in_specs=(spec, spec, spec, P(), P()),
        out_specs=spec,
        check_vma=False,
    )
```

```python
import jax
import jax.numpy as jnp
from jax import lax
from jax.experimental import pallas as pl
from jax.experimental.pallas import tpu as pltpu
from jax.sharding import PartitionSpec as P

HEAD = 128
LOG2E = 1.4426950408889634
BLOCK_Q = 384
KEY_STEP = 256
REACH = 5
CORES = 2
WEIGHT_LIMIT = 2.0**60
FIRST, KEEP, MOVE = range(3)


def fold(weight):
    best = weight[:, :HEAD]
    for j in range(HEAD, weight.shape[1], HEAD):
        best = jnp.maximum(best, weight[:, j : j + HEAD])
    while best.shape[0] % 32 == 0:
        half = best.shape[0] // 2
        best = jnp.maximum(best[:half], best[half:])
    tile = best[:16]
    for j in range(16, best.shape[0], 16):
        tile = jnp.maximum(tile, best[j : j + 16])
    return tile


def pack(queries, keys, values, slots):
    _, tokens, width = queries.shape
    parts = 4
    here = width // parts
    heads = here // HEAD

    def kernel(q_ref, k_ref, v_ref, o_ref, held, ready, in_sems, out_sems):
        def load(g, i):
            columns = slice(g * here, (g + 1) * here)
            return pltpu.make_async_copy((q_ref, k_ref, v_ref)[i].at[0, :, columns], held.at[g, i], in_sems.at[g, i])

        def store(g):
            return pltpu.make_async_copy(ready.at[g], o_ref.at[pl.ds(g * heads, heads)], out_sems.at[g])

        for g in range(parts):
            for i in range(3):
                load(g, i).start()
        for g in range(parts):
            for i in range(3):
                load(g, i).wait()
                for h in range(heads):
                    ready[g, h, i] = held[g, i, :, h * HEAD : (h + 1) * HEAD]
            store(g).start()
        for g in range(parts):
            store(g).wait()

    return pl.pallas_call(
        kernel,
        out_shape=jax.ShapeDtypeStruct((slots, 3, tokens, HEAD), queries.dtype),
        in_specs=[pl.BlockSpec(memory_space=pl.ANY)] * 3,
        out_specs=pl.BlockSpec(memory_space=pl.ANY),
        scratch_shapes=[
            pltpu.VMEM((parts, 3, tokens, here), queries.dtype),
            pltpu.VMEM((parts, heads, 3, tokens, HEAD), queries.dtype),
            pltpu.SemaphoreType.DMA((parts, 3)),
            pltpu.SemaphoreType.DMA((parts,)),
        ],
        compiler_params=pltpu.CompilerParams(vmem_limit_bytes=56 * 2**20),
        name="pack",
    )(queries, keys, values)


def tail(got):
    slots, kinds, tokens, _ = got.shape

    def kernel(got_ref, o_ref):
        def one(i, carry):
            for j in range(4):
                o_ref[i * 4 + j] = got_ref[i * 4 + j, 1:]
            return carry

        lax.fori_loop(0, slots // 4, one, 0)

    return pl.pallas_call(
        kernel,
        out_shape=jax.ShapeDtypeStruct((slots, kinds - 1, tokens, HEAD), got.dtype),
        in_specs=[pl.BlockSpec(memory_space=pltpu.VMEM)],
        out_specs=pl.BlockSpec(memory_space=pltpu.VMEM),
        compiler_params=pltpu.CompilerParams(vmem_limit_bytes=16 * 2**20),
        name="tail",
    )(got)


def unpack(back, heads):
    _, tokens, _ = back.shape

    def kernel(back_ref, o_ref, sems):
        copies = [
            pltpu.make_async_copy(back_ref.at[h], o_ref.at[0, :, h * HEAD : (h + 1) * HEAD], sems.at[h])
            for h in range(heads)
        ]
        for copy in copies:
            copy.start()
        for copy in copies:
            copy.wait()

    return pl.pallas_call(
        kernel,
        out_shape=jax.ShapeDtypeStruct((1, tokens, heads * HEAD), back.dtype),
        in_specs=[pl.BlockSpec(memory_space=pl.ANY)],
        out_specs=pl.BlockSpec(memory_space=pl.ANY),
        scratch_shapes=[pltpu.SemaphoreType.DMA((heads,))],
        compiler_params=pltpu.CompilerParams(vmem_limit_bytes=16 * 2**20),
        name="unpack",
    )(back)


def attend(lengths, span_mask, place, got, other):
    groups = span_mask.shape[0]
    run = got.shape[2]
    runs = got.shape[0] // groups
    rows = runs * run
    span = CORES * rows
    sizes = [n for n in range(KEY_STEP, span + 1, KEY_STEP) if n >= span // 2]

    def kernel(len_ref, mask_ref, place_ref, got_ref, other_ref, o_ref, q_in, keys, values, ones, q, top, acc, largest, sems):
        core = place_ref[1]
        by_run = (groups, runs, CORES, run, HEAD)
        keys_by_run, values_by_run = keys.reshape(by_run), values.reshape(by_run)

        def copies(c):
            here = pl.ds(c * runs, runs)
            pairs = (
                (got_ref.at[here, 0], q_in.at[c]),
                (got_ref.at[here, 1], keys_by_run.at[c, :, core]),
                (got_ref.at[here, 2], values_by_run.at[c, :, core]),
                (other_ref.at[here, 0], keys_by_run.at[c, :, 1 - core]),
                (other_ref.at[here, 1], values_by_run.at[c, :, 1 - core]),
            )
            return [pltpu.make_async_copy(src, dst, sems.at[c, i]) for i, (src, dst) in enumerate(pairs)]

        def start(c, carry):
            for copy in copies(c):
                copy.start()
            return carry

        def clean(c):
            count = len_ref[c]
            base = (count - 1) // KEY_STEP * KEY_STEP
            here = pl.ds(pl.multiple_of(c * span + base, KEY_STEP), KEY_STEP)
            live = (base + lax.broadcasted_iota(jnp.int32, (KEY_STEP, HEAD), 0)) < count
            first = keys[pl.ds(pl.multiple_of(c * span, KEY_STEP), 16), :][0:1]
            keys[here, :] = jnp.where(live, keys[here, :], first)
            values[here, :] = jnp.where(live, values[here, :], jnp.bfloat16(0))
            ones[here, :] = jnp.where(live, jnp.bfloat16(1), jnp.bfloat16(0))

        def step(c, n, kind):
            here = pl.ds(pl.multiple_of(c * span, KEY_STEP), n)
            k = keys[here, :]
            k = jnp.concatenate([k, k], axis=1)
            v = jnp.concatenate([values[here, :], ones[here, :]], axis=1)

            def scores(i):
                return lax.dot_general(
                    q[i * BLOCK_Q : (i + 1) * BLOCK_Q, :],
                    k,
                    (((1,), (1,)), ((), ())),
                    preferred_element_type=jnp.float32,
                )

            later = scores(0)
            for i in range(rows // BLOCK_Q):
                block = slice(i * BLOCK_Q, (i + 1) * BLOCK_Q)
                score = later
                if i + 1 < rows // BLOCK_Q:
                    later = scores(i + 1)
                if kind == KEEP:
                    kept = jnp.concatenate([top[block, :]] * (n // HEAD), axis=1)
                    weight = jnp.exp2(score - kept).astype(jnp.bfloat16)
                    largest[...] = jnp.maximum(largest[...], fold(weight))
                    acc[block, :] += jnp.dot(weight, v, preferred_element_type=jnp.float32)
                    continue
                new_top = jnp.max(score, axis=1, keepdims=True)
                if kind == MOVE:
                    old_top = top[block, 0:1]
                    new_top = jnp.maximum(old_top, new_top)
                weight = jnp.exp2(score - new_top).astype(jnp.bfloat16)
                update = jnp.dot(weight, v, preferred_element_type=jnp.float32)
                if kind == FIRST:
                    acc[block, :] = update
                else:
                    acc[block, :] = acc[block, :] * jnp.exp2(old_top - new_top) + update
                top[block, :] = jnp.broadcast_to(new_top, (BLOCK_Q, HEAD))

        def by_length(c, kind):
            steps = (len_ref[c] + KEY_STEP - 1) // KEY_STEP
            for n in sizes:
                pl.when(steps == n // KEY_STEP)(lambda n=n: step(c, n, kind))

        def one_group(s, carry):
            for copy in copies(s):
                copy.wait()
            clean(s)
            scaled = q_in[s].reshape(rows, HEAD).astype(jnp.float32) * (LOG2E * HEAD**-0.5)
            high = scaled.astype(jnp.bfloat16)
            q[:, :HEAD] = high
            q[:, HEAD:] = (scaled - high.astype(jnp.float32)).astype(jnp.bfloat16)

            def attempt(state):
                again, _ = state
                by_length(s, FIRST)
                largest[...] = jnp.zeros(largest.shape, jnp.bfloat16)

                def earlier(c, inner):
                    live = mask_ref[s, c] > 0
                    pl.when(live & (again == 0))(lambda: by_length(c, KEEP))
                    pl.when(live & (again > 0))(lambda: by_length(c, MOVE))
                    return inner

                lax.fori_loop(jnp.maximum(s - (REACH - 1), 0), s, earlier, 0)
                over = jnp.max(largest[...].astype(jnp.float32)) > WEIGHT_LIMIT
                return again + 1, over.astype(jnp.int32)

            zero = jnp.int32(0)
            lax.while_loop(lambda x: (x[0] == 0) | ((x[0] == 1) & (x[1] > 0)), attempt, (zero, zero))
            total = acc[...]
            o_ref[lax.rem(s + 1, groups)] = (total[:, :HEAD] / total[:, HEAD:]).astype(jnp.bfloat16)
            return carry

        @pl.when(place_ref[0] > 0)
        def _():
            lax.fori_loop(0, groups, start, 0)
            ones[...] = jnp.ones(ones.shape, jnp.bfloat16)
            lax.fori_loop(0, groups, one_group, 0)

    smem = pl.BlockSpec(memory_space=pltpu.SMEM)
    where_it_is = pl.BlockSpec(memory_space=pl.ANY)
    bf16, f32 = jnp.bfloat16, jnp.float32
    return pl.pallas_call(
        kernel,
        out_shape=jax.ShapeDtypeStruct((groups, rows, HEAD), bf16),
        in_specs=[smem] * 3 + [where_it_is] * 2,
        out_specs=pl.BlockSpec(memory_space=pltpu.VMEM),
        scratch_shapes=[
            pltpu.VMEM((groups, runs, run, HEAD), bf16),
            pltpu.VMEM((groups * span, HEAD), bf16),
            pltpu.VMEM((groups * span, HEAD), bf16),
            pltpu.VMEM((groups * span, HEAD), bf16),
            pltpu.VMEM((rows, 2 * HEAD), bf16),
            pltpu.VMEM((rows, HEAD), f32),
            pltpu.VMEM((rows, 2 * HEAD), f32),
            pltpu.VMEM((16, HEAD), bf16),
            pltpu.SemaphoreType.DMA((groups, 5)),
        ],
        compiler_params=pltpu.CompilerParams(vmem_limit_bytes=48 * 2**20),
        name="attend",
    )(lengths, span_mask, place, got, other)


CHIPS = ("xh", "z", "xl", "y")


def body(queries, keys, values, lengths, span_mask):
    tokens, width = queries.shape[1:]
    heads = width // HEAD
    chips = lax.axis_size(CHIPS)
    core = lax.axis_index("core")

    sent = pack(queries, keys, values, chips)
    got = lax.all_to_all(sent, CHIPS, 0, 0, tiled=True)

    other = lax.ppermute(tail(got), "core", [(0, 1), (1, 0)])
    active = (lax.axis_index(CHIPS) < heads).astype(jnp.int32)
    out = attend(lengths, span_mask, jnp.stack([active, core]), got, other)
    back = lax.all_to_all(out.reshape(chips, tokens, HEAD), CHIPS, 0, 0, tiled=True)
    return unpack(back, heads)


def solution(mesh):
    fine = jax.sharding.Mesh(mesh.devices.reshape(2, 4, 2, 4, 2), ("xh", "z", "xl", "y", "core"))
    spec = P(("xh", "z"), ("xl", "y", "core"), None)
    return jax.shard_map(
        body,
        mesh=fine,
        in_specs=(spec, spec, spec, P(), P()),
        out_specs=spec,
        check_vma=False,
    )
```
